32 devices in a mesh: groups: 2 (over x), dev: 8 (over z, y), rve: 2 (over core).
Axes of the slice: x: 2, y: 2, z: 4, core: 2. Of those that a mesh axis runs over, the one named last changes fastest.
Arguments:
- phase: int32 [4, 64, 128, 128], P(('groups', 'rve'), 'dev'), parts along dimension 0, may hold values from 0 to 2
- load_case: int32 [4], P(('groups', 'rve')), parts along dimension 0, may hold values from 0 to 5
- moduli: float32 [2, 3], replicated, may hold values from 0.5 to 8
- loading_table: float32 [6, 3, 3], replicated, may hold values from -4 to 4
- w_embed: bfloat16 [1408, 768], P(('dev', 'rve')), may hold values from -0.21875 to 0.21875
- w_up: bfloat16 [3072, 1408], P(('dev', 'rve')), may hold values from -0.15625 to 0.15625
- cotangent: bfloat16 [16384, 3072], P(('groups', 'dev', 'rve')), parts along dimension 0, may hold values from -6 to 6
Outputs:
- displacement: float32 [4, 3, 64, 128, 128], P(('groups', 'rve'), None, 'dev'), parts along dimension 0
- grad_embed: float32 [2816, 768], P(('groups', 'dev', 'rve')), parts along dimension 0
- grad_up: float32 [6144, 1408], P(('groups', 'dev', 'rve')), parts along dimension 0
The draws below stay inside these ranges and needn't reach their ends.
There are 2 independent parts, one for each index of `groups`. The reference program is written for one: setup_inputs(seed, part) draws one part's arguments, and reference() takes and returns one part's arrays. A program takes and returns all parts, laid end to end along the dimension named above; an argument that names none is the same for every part. Nothing has to cross between parts.
Inputs may be any that keep to these rules, and one draw needn't show every extreme that they name: `load_case`: row of loading_table for each RVE.
All inputs are finite; a program needn't handle non-finite values.
Results may differ from the reference program's by a relative error of at most 0.0069.
Values may be sent and summed in bfloat16 or wider, within the bound.
A program may use at most 128 MiB of HBM per device.

```python
import math
from functools import partial
import jax
import jax.numpy as jnp
from jax import lax

D = 1408
FF = 3072
PATCH_X = 8
PATCH_Y = 8
PATCH_Z = 4
FEATURES = 768
NY = 128
NZ = 128
SWEEPS = 4
PHASES = 3
CASES = 6
NX = 64
RVES = 2
TOKENS = 8192
N_DEV = 8


def set_ends(array, stream_key, least, top_value):
    dims = array.shape
    place = [jax.random.randint(jax.random.fold_in(stream_key, axis), (), 0, dims[axis]) for axis in range(len(dims))]
    array = array.at[tuple(place)].set(least)
    longest = dims.index(max(dims))
    place[longest] = (place[longest] + 1) % dims[longest]
    return array.at[tuple(place)].set(top_value)


def strengthened(entries, key, source, target, shards_of, factor):
    owner, partner = [(jnp.arange(entries.shape[dim]) // (entries.shape[dim] // shards_of)).reshape([-1 if axis == dim else 1 for axis in range(entries.ndim)]) for dim in (source, target)]
    chosen = jax.random.permutation(key, shards_of)[partner]
    strong = (owner == chosen) | (owner == (partner + shards_of // 2) % shards_of)
    return jnp.where(strong, factor * entries, entries)


def steps_of(own_key, shape, cuts, least, largest):
    def one(position, parts):
        draws = jax.random.uniform(jax.random.fold_in(jax.random.fold_in(own_key, 6), position), (parts,), jnp.float32, least / len(cuts), largest / len(cuts))
        return jnp.repeat(jnp.exp(draws), shape[position] // parts).reshape((-1,) + (1,) * (len(shape) - position - 1))

    factor_of = one(*cuts[0])
    for cut in cuts[1:]:
        factor_of = factor_of * one(*cut)
    return factor_of


def centred(rng, extent, deviation, bound, pieces=(), kind=jnp.bfloat16):
    result = jax.random.normal(rng, extent, jnp.float32) * deviation
    if len(pieces) > 0:
        result = steps_of(rng, extent, pieces, -0.22, 0.18) * result
    return jnp.clip(result, min=-bound, max=bound).astype(kind)


def noise_with(key, extent, spread, reach, split, heavy, kind=jnp.bfloat16):
    values = spread * jax.random.normal(key, extent, jnp.float32)
    if split:
        values = values * steps_of(key, extent, split, -0.22, 0.18)
    return jnp.clip(strengthened(values, jax.random.fold_in(key, 3), *heavy), -reach, reach).astype(kind)


def setup_inputs(seed: int = 0, part: int = 0) -> dict:
    key_of = jax.random.split(jax.random.key(seed), 8)
    part_splits = jax.random.split(jax.random.fold_in(key_of[7], part), 8)
    return {
        "phase": set_ends(jax.random.randint(part_splits[0], (RVES, NX, NY, NZ), 0, PHASES), jax.random.fold_in(part_splits[0], 1), 0, PHASES - 1).astype(jnp.int32),
        "load_case": jax.random.randint(part_splits[1], (RVES,), 0, CASES).astype(jnp.int32),
        "moduli": jnp.clip(jnp.exp(jax.random.uniform(key_of[2], (2, PHASES), jnp.float32, math.log(0.5), math.log(8.0))), 0.5, 8.0),
        "loading_table": centred(key_of[3], (CASES, 3, 3), 1.0, 4.0, (), jnp.float32),
        "w_embed": centred(key_of[4], (D, FEATURES), FEATURES ** -0.5, 0.21875, ((0, 16),)),
        "w_up": centred(key_of[5], (FF, D), D ** -0.5, 0.15625, ((0, 16),)),
        "cotangent": noise_with(part_splits[6], (TOKENS, FF), 1.0, 6.0, ((0, 16),), (0, 1, 16, 2.0)),
    }


epsilon = 1e-06

def stiffness(phase, moduli):
    labels = jnp.arange(moduli.shape[1], dtype=jnp.int32)
    member = (labels[:, None, None, None] == phase[None]).astype(jnp.float32)
    shear_stiff = lax.optimization_barrier(jnp.sum(member * moduli[0][:, None, None, None], axis=0))
    axial_stiff = lax.optimization_barrier(jnp.sum(member * moduli[1][:, None, None, None], axis=0))
    return (shear_stiff, axial_stiff)

def harmonic(here, there, in_here, in_there):
    blended = 2.0 * here * there / (here + there)
    return jnp.where(in_here & in_there, blended, jnp.where(in_here, here, there))

def face_pairs(stiff, inside):
    stiff = jnp.where(inside, stiff, 1.0)
    padded = jnp.pad(stiff, 1, constant_values=1.0)
    in_pad = jnp.pad(inside, 1)
    face_list = []
    for direction in range(3):
        upper_cut = [slice(1, -1)] * 3
        lower_cut = [slice(1, -1)] * 3
        upper_cut[direction] = slice(2, None)
        lower_cut[direction] = slice(0, -2)
        upper_face = harmonic(stiff, padded[tuple(upper_cut)], inside, in_pad[tuple(upper_cut)])
        lower_face = harmonic(stiff, padded[tuple(lower_cut)], inside, in_pad[tuple(lower_cut)])
        face_list.append((upper_face, lower_face))
    return face_list

def operator_terms(shear_stiff, axial_stiff, inside, strain):
    shear_faces = face_pairs(shear_stiff, inside)
    axial_faces = face_pairs(axial_stiff, inside)
    terms = []
    for component in range(3):
        face_list = [axial_faces[direction] if direction == component else shear_faces[direction] for direction in range(3)]
        forcing = strain[component, 0] * (face_list[0][0] - face_list[0][1])
        diagonal = face_list[0][0] + face_list[0][1]
        for direction in (1, 2):
            forcing = forcing + strain[component, direction] * (face_list[direction][0] - face_list[direction][1])
            diagonal = diagonal + face_list[direction][0] + face_list[direction][1]
        terms.append((face_list, forcing, diagonal))
    return terms

def first_iterate(terms, inside):
    return jnp.stack([jnp.where(inside, forcing / diagonal, 0.0) for face_list, forcing, diagonal in terms])

def jacobi_sweep(ghosted, terms, inside):
    results = []
    for component in range(3):
        face_list, forcing, diagonal = terms[component]
        padded = jnp.pad(ghosted[component], ((0, 0), (1, 1), (1, 1)))
        summed = forcing
        for direction in range(3):
            upper_cut = [slice(1, -1)] * 3
            lower_cut = [slice(1, -1)] * 3
            upper_cut[direction] = slice(2, None)
            lower_cut[direction] = slice(0, -2)
            summed = summed + face_list[direction][0] * padded[tuple(upper_cut)] + face_list[direction][1] * padded[tuple(lower_cut)]
        results.append(jnp.where(inside, summed / diagonal, 0.0))
    return jnp.stack(results)

def gelu_grad(pre_act, cotangent):
    _, pullback = jax.vjp(partial(jax.nn.gelu, approximate=True), pre_act)
    return pullback(cotangent.astype(jnp.float32))[0].astype(jnp.bfloat16)

def reference(phase, load_case, moduli, loading_table, w_embed, w_up, cotangent):
    fields = []
    for member_index in range(RVES):
        shear_stiff, axial_stiff = stiffness(phase[member_index], moduli)
        strain = loading_table[load_case[member_index]]
        inside = jnp.ones(phase.shape[1:], dtype=bool)
        terms = operator_terms(shear_stiff, axial_stiff, inside, strain)
        displace = first_iterate(terms, inside)
        for repeat in range(SWEEPS - 1):
            displace = jacobi_sweep(jnp.pad(displace, ((0, 0), (1, 1), (0, 0), (0, 0))), terms, inside)
        fields.append(displace)
    displacement = jnp.stack(fields)
    cells = displacement.astype(jnp.bfloat16).reshape(RVES, 3, NX // PATCH_X, PATCH_X, N_DEV, NY // (N_DEV * PATCH_Y), PATCH_Y, NZ // PATCH_Z, PATCH_Z)
    patches = cells.transpose(4, 0, 5, 2, 7, 1, 3, 6, 8).reshape(TOKENS, FEATURES)
    grad_scale = 1.0 / math.sqrt(TOKENS)
    embedded = jnp.dot(patches, w_embed.T, preferred_element_type=jnp.float32).astype(jnp.bfloat16)
    embed_wide = embedded.astype(jnp.float32)
    inverse_rms = lax.rsqrt(lax.optimization_barrier(jnp.mean(embed_wide * embed_wide, axis=-1, keepdims=True)) + epsilon)
    normed_wide = embed_wide * inverse_rms
    normed = normed_wide.astype(jnp.bfloat16)
    pre_act = jnp.dot(normed, w_up.T, preferred_element_type=jnp.float32)
    act_grad = gelu_grad(pre_act, cotangent)
    grad_up = jnp.dot(act_grad.T, normed, preferred_element_type=jnp.float32) * grad_scale
    normed_grad = jnp.dot(act_grad, w_up, preferred_element_type=jnp.float32)
    embed_in_grad = (inverse_rms * (normed_grad - normed_wide * lax.optimization_barrier(jnp.mean(normed_grad * normed_wide, axis=-1, keepdims=True)))).astype(jnp.bfloat16)
    grad_embed = jnp.dot(embed_in_grad.T, patches, preferred_element_type=jnp.float32) * grad_scale
    return (displacement, grad_embed, grad_up)
```

```python
from functools import partial
import math

import jax
import jax.numpy as jnp
from jax import lax
from jax.experimental import pallas as pl
from jax.experimental.pallas import tpu as pltpu
from jax.sharding import PartitionSpec as P

PATCH_X = 8
PATCH_Y = 8
PATCH_Z = 4
SWEEPS = 4


epsilon = 1e-06


def with_halo(value, sides, width):
    for axis, dim in sides:
        size, length = (lax.axis_size(axis), value.shape[dim])
        up = [(i, (i + 1) % size) for i in range(size - 1)]
        down = [(j, i) for i, j in up]
        last = lax.slice_in_dim(value, length - width, length, axis=dim)
        initial = lax.slice_in_dim(value, 0, width, axis=dim)
        before = lax.ppermute(last, axis, up)
        after = lax.ppermute(initial, axis, down)
        value = jnp.concatenate([before, value, after], axis=dim)
    return value


def stiffness(phase, moduli):
    labels = jnp.arange(moduli.shape[1], dtype=jnp.int32)
    member = (labels[:, None, None, None] == phase[None]).astype(jnp.float32)
    shear_stiff = jnp.sum(member * moduli[0][:, None, None, None], axis=0)
    axial_stiff = jnp.sum(member * moduli[1][:, None, None, None], axis=0)
    return (shear_stiff, axial_stiff)


def harmonic(here, there, in_here, in_there):
    blended = 2.0 * here * there / (here + there)
    return jnp.where(in_here & in_there, blended, jnp.where(in_here, here, there))


def face_pairs(stiff, inside):
    stiff = jnp.where(inside, stiff, 1.0)
    padded = jnp.pad(stiff, 1, constant_values=1.0)
    in_pad = jnp.pad(inside, 1)
    face_list = []
    for direction in range(3):
        upper_cut = [slice(1, -1)] * 3
        lower_cut = [slice(1, -1)] * 3
        upper_cut[direction] = slice(2, None)
        lower_cut[direction] = slice(0, -2)
        upper_face = harmonic(stiff, padded[tuple(upper_cut)], inside, in_pad[tuple(upper_cut)])
        lower_face = harmonic(stiff, padded[tuple(lower_cut)], inside, in_pad[tuple(lower_cut)])
        face_list.append((upper_face, lower_face))
    return face_list


def operator_terms(shear_stiff, axial_stiff, inside, strain):
    shear_faces = face_pairs(shear_stiff, inside)
    axial_faces = face_pairs(axial_stiff, inside)
    terms = []
    for component in range(3):
        face_list = [
            axial_faces[direction] if direction == component else shear_faces[direction]
            for direction in range(3)
        ]
        forcing = strain[component, 0] * (face_list[0][0] - face_list[0][1])
        diagonal = face_list[0][0] + face_list[0][1]
        for direction in (1, 2):
            forcing = forcing + strain[component, direction] * (
                face_list[direction][0] - face_list[direction][1]
            )
            diagonal = diagonal + face_list[direction][0] + face_list[direction][1]
        terms.append((face_list, forcing, diagonal))
    return terms


def first_iterate(terms, inside):
    return jnp.stack(
        [jnp.where(inside, forcing / diagonal, 0.0) for face_list, forcing, diagonal in terms]
    )


def jacobi_sweep(ghosted, terms, inside):
    results = []
    for component in range(3):
        face_list, forcing, diagonal = terms[component]
        padded = jnp.pad(ghosted[component], ((0, 0), (1, 1), (1, 1)))
        summed = forcing
        for direction in range(3):
            upper_cut = [slice(1, -1)] * 3
            lower_cut = [slice(1, -1)] * 3
            upper_cut[direction] = slice(2, None)
            lower_cut[direction] = slice(0, -2)
            summed = (
                summed
                + face_list[direction][0] * padded[tuple(upper_cut)]
                + face_list[direction][1] * padded[tuple(lower_cut)]
            )
        results.append(jnp.where(inside, summed / diagonal, 0.0))
    return jnp.stack(results)


def row_mask(first_global, row_total, grid_rows, plane_shape):
    global_rows = first_global + jnp.arange(row_total, dtype=jnp.int32)
    within = (global_rows >= 0) & (global_rows < grid_rows)
    return jnp.broadcast_to(within[:, None, None], (row_total,) + tuple(plane_shape))


MESH = pl.DeviceIdType.MESH
LANES = 128


def dot_last(left, right):
    return lax.dot_general(
        left, right, (((1,), (1,)), ((), ())), preferred_element_type=jnp.float32
    )


def ring_place(dev, size):
    odd = dev % 2
    return (1 - odd) * (dev // 2) + odd * (size - 1 - dev // 2)


def ring_dev(place, size):
    back = place // (size // 2)
    return (1 - back) * (2 * place) + back * (2 * (size - 1 - place) + 1)


def scatter_kernel(
    size, scale, up_cut, embed_cut,
    act_ref, normed_ref, embed_ref, patch_ref, up_out, embed_out,
    own_up, own_em, pair_out_up, pair_out_em, pair_in_up, pair_in_em,
    ring_out_up, ring_out_em, ring_in_up, ring_in_em,
    pair_send, pair_recv, ring_send, ring_recv,
):
    dev = lax.axis_index("dev")
    core = lax.axis_index("rve")
    place = ring_place(dev, size)
    right = ring_dev((place + 1) % size, size)
    left = ring_dev((place + size - 1) % size, size)
    barrier = pltpu.get_barrier_semaphore()
    pl.semaphore_signal(barrier, inc=1, device_id={"dev": right}, device_id_type=MESH)
    pl.semaphore_signal(barrier, inc=1, device_id={"dev": left}, device_id_type=MESH)
    pl.semaphore_signal(barrier, inc=1, device_id={"rve": 1 - core}, device_id_type=MESH)
    pl.semaphore_wait(barrier, 3)
    sides = (
        (slice(0, up_cut), slice(0, embed_cut)),
        (slice(up_cut, None), slice(embed_cut, None)),
    )

    def pair_copies(step):
        return [
            pltpu.make_async_remote_copy(
                src_ref=source.at[step], dst_ref=target.at[step],
                send_sem=pair_send.at[kind, step], recv_sem=pair_recv.at[kind, step],
                device_id={"rve": 1 - core}, device_id_type=MESH,
            )
            for kind, (source, target) in enumerate(
                ((pair_out_up, pair_in_up), (pair_out_em, pair_in_em))
            )
        ]

    def ring_copies(step):
        copies = []
        for side, neighbour in enumerate((right, left)):
            for kind, (source, target) in enumerate(
                ((ring_out_up, ring_in_up), (ring_out_em, ring_in_em))
            ):
                cut = sides[side][kind]
                copies.append(
                    pltpu.make_async_remote_copy(
                        src_ref=source.at[step, :, cut], dst_ref=target.at[step, :, cut],
                        send_sem=ring_send.at[2 * side + kind, step],
                        recv_sem=ring_recv.at[2 * side + kind, step],
                        device_id={"dev": neighbour}, device_id_type=MESH,
                    )
                )
        return copies

    def compute(step):
        blocks = ((place + 2 * size - 1 - step) % size, (place + 1 + step) % size)
        for other in (True, False):
            for side in range(2):
                up_cols, em_cols = sides[side]
                block = ring_dev(blocks[side], size) * 2 + ((1 - core) if other else core)
                up = dot_last(act_ref[block], normed_ref[up_cols])
                em = dot_last(embed_ref[block], patch_ref[em_cols])
                if other:
                    pair_out_up[step, :, up_cols] = up.astype(jnp.bfloat16)
                    pair_out_em[step, :, em_cols] = em.astype(jnp.bfloat16)
                else:
                    own_up[step % 2, :, up_cols] = up
                    own_em[step % 2, :, em_cols] = em
            if other:
                for copy in pair_copies(step):
                    copy.start()

    def finish(step, first, last):
        for copy in pair_copies(step):
            copy.wait_recv()
        up = own_up[step % 2] + pair_in_up[step].astype(jnp.float32)
        em = own_em[step % 2] + pair_in_em[step].astype(jnp.float32)
        if not first:
            for copy in ring_copies(step - 1):
                copy.wait_recv()
            up = up + ring_in_up[step - 1].astype(jnp.float32)
            em = em + ring_in_em[step - 1].astype(jnp.float32)
        if last:
            up_out[...] = up * scale
            embed_out[...] = em * scale
        else:
            ring_out_up[step] = up.astype(jnp.bfloat16)
            ring_out_em[step] = em.astype(jnp.bfloat16)
            for copy in ring_copies(step):
                copy.start()

    compute(0)
    compute(1)
    finish(0, True, False)

    def body(step, carry):
        compute(step + 1)
        finish(step, False, False)
        return carry

    lax.fori_loop(1, size - 1, body, 0)
    finish(size - 1, False, True)

    def drain(step, carry):
        for copy in pair_copies(step):
            copy.wait_send()
        return carry

    def drain_ring(step, carry):
        for copy in ring_copies(step):
            copy.wait_send()
        return carry

    lax.fori_loop(0, size, drain, 0)
    lax.fori_loop(0, size - 1, drain_ring, 0)


def scatter_grads(act, normed, embed, patches, scale, size):
    up_rows, em_rows = act.shape[1], embed.shape[1]
    width, features = normed.shape[0], patches.shape[0]
    up_cut = (width // LANES + 1) // 2 * LANES
    embed_cut = features // LANES // 3 * LANES
    wide = jnp.bfloat16
    return pl.pallas_call(
        partial(scatter_kernel, size, scale, up_cut, embed_cut),
        out_shape=(
            jax.ShapeDtypeStruct((up_rows, width), jnp.float32),
            jax.ShapeDtypeStruct((em_rows, features), jnp.float32),
        ),
        in_specs=[pl.BlockSpec(memory_space=pltpu.VMEM)] * 4,
        out_specs=(pl.BlockSpec(memory_space=pltpu.VMEM),) * 2,
        scratch_shapes=[
            pltpu.VMEM((2, up_rows, width), jnp.float32),
            pltpu.VMEM((2, em_rows, features), jnp.float32),
            *[
                pltpu.VMEM(shape, wide)
                for _ in range(4)
                for shape in ((size, up_rows, width), (size, em_rows, features))
            ],
            pltpu.SemaphoreType.DMA((2, size)),
            pltpu.SemaphoreType.DMA((2, size)),
            pltpu.SemaphoreType.DMA((4, size)),
            pltpu.SemaphoreType.DMA((4, size)),
        ],
        compiler_params=pltpu.CompilerParams(
            collective_id=0, has_side_effects=True, vmem_limit_bytes=58 * 1024 * 1024
        ),
        cost_estimate=pl.CostEstimate(
            flops=4 * size * patches.shape[1] * (up_rows * width + em_rows * features),
            bytes_accessed=20_000_000,
            transcendentals=0,
        ),
    )(act, normed, embed, patches)


def gelu_grad(pre_act, cotangent):
    _, pullback = jax.vjp(partial(jax.nn.gelu, approximate=True), pre_act)
    return pullback(cotangent.astype(jnp.float32))[0].astype(jnp.bfloat16)


def learner(patches, embed_all, up_all, cotangent, dev_count, rve_count):
    tokens = patches.shape[1]
    shards = dev_count * rve_count
    grad_scale = 1.0 / math.sqrt(tokens * shards)
    embedded = jnp.dot(embed_all, patches, preferred_element_type=jnp.float32).astype(jnp.bfloat16)
    embed_wide = embedded.astype(jnp.float32)
    inverse_rms = lax.rsqrt(jnp.mean(embed_wide * embed_wide, axis=0, keepdims=True) + epsilon)
    normed_wide = embed_wide * inverse_rms
    normed = normed_wide.astype(jnp.bfloat16)
    pre_act = jnp.dot(up_all, normed, preferred_element_type=jnp.float32)
    act_grad = gelu_grad(pre_act, cotangent)
    normed_grad = lax.dot_general(
        up_all, act_grad, (((0,), (0,)), ((), ())), preferred_element_type=jnp.float32
    )
    embed_in_grad = (
        inverse_rms
        * (normed_grad - normed_wide * jnp.mean(normed_grad * normed_wide, axis=0, keepdims=True))
    ).astype(jnp.bfloat16)
    grad_up, grad_embed = scatter_grads(
        act_grad.reshape(shards, -1, tokens),
        normed,
        embed_in_grad.reshape(shards, -1, tokens),
        patches,
        grad_scale,
        dev_count,
    )
    return (grad_embed, grad_up)


def local(phase, load_case, moduli, loading_table, w_embed, w_up, cotangent):
    local_phase = phase[0]
    slab_rows = local_phase.shape[0]
    plane_shape = local_phase.shape[1:]
    dev_count = lax.axis_size("dev")
    rve_count = lax.axis_size("rve")
    first_row = lax.axis_index("dev") * slab_rows
    grid_rows = slab_rows * dev_count
    shear_stiff, axial_stiff = stiffness(local_phase, moduli)
    case_labels = jnp.arange(loading_table.shape[0], dtype=jnp.int32)
    case_pick = (case_labels == load_case[0]).astype(jnp.float32)
    strain = jnp.sum(case_pick[:, None, None] * loading_table, axis=0)
    stacked = jnp.stack([shear_stiff, axial_stiff])
    ghosted = with_halo(stacked, (("dev", 1),), SWEEPS)
    inside = row_mask(first_row - SWEEPS, slab_rows + 2 * SWEEPS, grid_rows, plane_shape)
    terms = operator_terms(ghosted[0], ghosted[1], inside, strain)
    displace = first_iterate(terms, inside)
    for repeat in range(SWEEPS - 1):
        displace = jacobi_sweep(jnp.pad(displace, ((0, 0), (1, 1), (0, 0), (0, 0))), terms, inside)
    displace = displace[:, SWEEPS : SWEEPS + slab_rows]
    rounded = displace.astype(jnp.bfloat16)
    ny_cells = rounded.shape[2]
    nz_cells = rounded.shape[3]
    band_rows = ny_cells // dev_count
    blocks = rounded.reshape(3, slab_rows, dev_count, band_rows, nz_cells)
    regrouped = lax.all_to_all(blocks, "dev", split_axis=2, concat_axis=1, tiled=True)
    grid_x = regrouped.shape[1]
    cells = regrouped.reshape(
        3, grid_x // PATCH_X, PATCH_X, band_rows // PATCH_Y, PATCH_Y, nz_cells // PATCH_Z, PATCH_Z
    )
    patches = cells.transpose(3, 1, 5, 0, 2, 4, 6).reshape(-1, 3 * PATCH_X * PATCH_Y * PATCH_Z)
    return (displace[None],) + learner(
        patches.T,
        lax.all_gather(w_embed, ("dev", "rve"), axis=0, tiled=True),
        lax.all_gather(w_up, ("dev", "rve"), axis=0, tiled=True),
        cotangent.T,
        dev_count,
        rve_count,
    )


def solution(mesh):
    return jax.shard_map(
        local,
        mesh=mesh,
        in_specs=(
            P(("groups", "rve"), "dev", None, None),
            P(("groups", "rve")),
            P(),
            P(),
            P(("dev", "rve"), None),
            P(("dev", "rve"), None),
            P(("groups", "dev", "rve"), None),
        ),
        out_specs=(
            P(("groups", "rve"), None, "dev", None, None),
            P(("groups", "dev", "rve"), None),
            P(("groups", "dev", "rve"), None),
        ),
        check_vma=False,
    )
```

```python
from functools import partial
import math

import jax
import jax.numpy as jnp
from jax import lax
from jax.experimental import pallas as pl
from jax.experimental.pallas import tpu as pltpu
from jax.sharding import PartitionSpec as P

PATCH_X = 8
PATCH_Y = 8
PATCH_Z = 4
SWEEPS = 4


epsilon = 1e-06


MESH = pl.DeviceIdType.MESH
LANES = 128


def dot_last(left, right):
    return lax.dot_general(
        left, right, (((1,), (1,)), ((), ())), preferred_element_type=jnp.float32
    )


def ring_place(dev, size):
    odd = dev % 2
    return (1 - odd) * (dev // 2) + odd * (size - 1 - dev // 2)


def ring_dev(place, size):
    back = place // (size // 2)
    return (1 - back) * (2 * place) + back * (2 * (size - 1 - place) + 1)


def scatter_kernel(
    size, scale, up_cut, embed_cut,
    act_ref, normed_ref, embed_ref, patch_ref, up_out, embed_out,
    own_up, own_em, pair_out_up, pair_out_em, pair_in_up, pair_in_em,
    ring_out_up, ring_out_em, ring_in_up, ring_in_em,
    pair_send, pair_recv, ring_send, ring_recv,
):
    dev = lax.axis_index("dev")
    core = lax.axis_index("rve")
    place = ring_place(dev, size)
    right = ring_dev((place + 1) % size, size)
    left = ring_dev((place + size - 1) % size, size)
    barrier = pltpu.get_barrier_semaphore()
    pl.semaphore_signal(barrier, inc=1, device_id={"dev": right}, device_id_type=MESH)
    pl.semaphore_signal(barrier, inc=1, device_id={"dev": left}, device_id_type=MESH)
    pl.semaphore_signal(barrier, inc=1, device_id={"rve": 1 - core}, device_id_type=MESH)
    pl.semaphore_wait(barrier, 3)
    sides = (
        (slice(0, up_cut), slice(0, embed_cut)),
        (slice(up_cut, None), slice(embed_cut, None)),
    )

    def pair_copies(step):
        return [
            pltpu.make_async_remote_copy(
                src_ref=source.at[step], dst_ref=target.at[step],
                send_sem=pair_send.at[kind, step], recv_sem=pair_recv.at[kind, step],
                device_id={"rve": 1 - core}, device_id_type=MESH,
            )
            for kind, (source, target) in enumerate(
                ((pair_out_up, pair_in_up), (pair_out_em, pair_in_em))
            )
        ]

    def ring_copies(step):
        copies = []
        for side, neighbour in enumerate((right, left)):
            for kind, (source, target) in enumerate(
                ((ring_out_up, ring_in_up), (ring_out_em, ring_in_em))
            ):
                cut = sides[side][kind]
                copies.append(
                    pltpu.make_async_remote_copy(
                        src_ref=source.at[step, :, cut], dst_ref=target.at[step, :, cut],
                        send_sem=ring_send.at[2 * side + kind, step],
                        recv_sem=ring_recv.at[2 * side + kind, step],
                        device_id={"dev": neighbour}, device_id_type=MESH,
                    )
                )
        return copies

    def compute(step):
        blocks = ((place + 2 * size - 1 - step) % size, (place + 1 + step) % size)
        for other in (True, False):
            for side in range(2):
                up_cols, em_cols = sides[side]
                block = ring_dev(blocks[side], size) * 2 + ((1 - core) if other else core)
                up = dot_last(act_ref[block], normed_ref[up_cols])
                em = dot_last(embed_ref[block], patch_ref[em_cols])
                if other:
                    pair_out_up[step, :, up_cols] = up.astype(jnp.bfloat16)
                    pair_out_em[step, :, em_cols] = em.astype(jnp.bfloat16)
                else:
                    own_up[step % 2, :, up_cols] = up
                    own_em[step % 2, :, em_cols] = em
            if other:
                for copy in pair_copies(step):
                    copy.start()

    def finish(step, first, last):
        for copy in pair_copies(step):
            copy.wait_recv()
        up = own_up[step % 2] + pair_in_up[step].astype(jnp.float32)
        em = own_em[step % 2] + pair_in_em[step].astype(jnp.float32)
        if not first:
            for copy in ring_copies(step - 1):
                copy.wait_recv()
            up = up + ring_in_up[step - 1].astype(jnp.float32)
            em = em + ring_in_em[step - 1].astype(jnp.float32)
        if last:
            up_out[...] = up * scale
            embed_out[...] = em * scale
        else:
            ring_out_up[step] = up.astype(jnp.bfloat16)
            ring_out_em[step] = em.astype(jnp.bfloat16)
            for copy in ring_copies(step):
                copy.start()

    compute(0)
    compute(1)
    finish(0, True, False)

    def body(step, carry):
        compute(step + 1)
        finish(step, False, False)
        return carry

    lax.fori_loop(1, size - 1, body, 0)
    finish(size - 1, False, True)

    def drain(step, carry):
        for copy in pair_copies(step):
            copy.wait_send()
        return carry

    def drain_ring(step, carry):
        for copy in ring_copies(step):
            copy.wait_send()
        return carry

    lax.fori_loop(0, size, drain, 0)
    lax.fori_loop(0, size - 1, drain_ring, 0)


def scatter_grads(act, normed, embed, patches, scale, size):
    up_rows, em_rows = act.shape[1], embed.shape[1]
    width, features = normed.shape[0], patches.shape[0]
    up_cut = (width // LANES + 1) // 2 * LANES
    embed_cut = features // LANES // 3 * LANES
    wide = jnp.bfloat16
    return pl.pallas_call(
        partial(scatter_kernel, size, scale, up_cut, embed_cut),
        out_shape=(
            jax.ShapeDtypeStruct((up_rows, width), jnp.float32),
            jax.ShapeDtypeStruct((em_rows, features), jnp.float32),
        ),
        in_specs=[pl.BlockSpec(memory_space=pltpu.VMEM)] * 4,
        out_specs=(pl.BlockSpec(memory_space=pltpu.VMEM),) * 2,
        scratch_shapes=[
            pltpu.VMEM((2, up_rows, width), jnp.float32),
            pltpu.VMEM((2, em_rows, features), jnp.float32),
            *[
                pltpu.VMEM(shape, wide)
                for _ in range(4)
                for shape in ((size, up_rows, width), (size, em_rows, features))
            ],
            pltpu.SemaphoreType.DMA((2, size)),
            pltpu.SemaphoreType.DMA((2, size)),
            pltpu.SemaphoreType.DMA((4, size)),
            pltpu.SemaphoreType.DMA((4, size)),
        ],
        compiler_params=pltpu.CompilerParams(
            collective_id=0, has_side_effects=True, vmem_limit_bytes=58 * 1024 * 1024
        ),
        cost_estimate=pl.CostEstimate(
            flops=4 * size * patches.shape[1] * (up_rows * width + em_rows * features),
            bytes_accessed=20_000_000,
            transcendentals=0,
        ),
    )(act, normed, embed, patches)


def gelu_grad(pre_act, cotangent):
    _, pullback = jax.vjp(partial(jax.nn.gelu, approximate=True), pre_act)
    return pullback(cotangent.astype(jnp.float32))[0].astype(jnp.bfloat16)


def field_kernel(
    size, grid_rows, phase_ref, inverse_ref, strain_ref, up_ref, em_ref,
    disp_ref, patch_ref, up_all, em_all,
    labels, face_x, face_y, face_z, forcing, scale_back, field, outgo, income, sorted_rows,
    halo_send, halo_recv, ring_send, ring_recv, pair_send, pair_recv, own_sem, swap_send, swap_recv,
):
    slab, ny, nz = phase_ref.shape
    width = SWEEPS
    phases = inverse_ref.shape[1]
    dev = lax.axis_index("dev")
    core = lax.axis_index("rve")
    place = ring_place(dev, size)
    right = ring_dev((place + 1) % size, size)
    left = ring_dev((place + size - 1) % size, size)
    half = size // 2
    up_cut = (up_ref.shape[1] // LANES + 1) // 2 * LANES
    em_cut = em_ref.shape[1] // LANES // 3 * LANES

    barrier = pltpu.get_barrier_semaphore()
    for offset in range(1, size):
        pl.semaphore_signal(
            barrier, inc=1, device_id={"dev": (dev + offset) % size}, device_id_type=MESH
        )
    pl.semaphore_signal(barrier, inc=1, device_id={"rve": 1 - core}, device_id_type=MESH)
    pl.semaphore_wait(barrier, size)

    def halo(up):
        if up:
            source, target = phase_ref.at[pl.ds(slab - width, width)], labels.at[pl.ds(0, width)]
        else:
            source, target = phase_ref.at[pl.ds(0, width)], labels.at[pl.ds(width + slab, width)]
        way = 0 if up else 1
        return pltpu.make_async_remote_copy(
            src_ref=source, dst_ref=target, send_sem=halo_send.at[way], recv_sem=halo_recv.at[way],
            device_id={"dev": (dev + 1) % size if up else (dev + size - 1) % size},
            device_id_type=MESH,
        )

    @pl.when(dev < size - 1)
    def _():
        halo(True).start()

    @pl.when(dev > 0)
    def _():
        halo(False).start()

    def index_of(spot):
        return ring_dev((spot + 2 * size) % size, size) * 2 + core

    def ring_copies(step):
        copies = []
        for side, neighbour in enumerate((right, left)):
            spot = place - step if side == 0 else place + step
            block = index_of(spot)
            for kind, (mine, every, cut) in enumerate(
                ((up_ref, up_all, up_cut), (em_ref, em_all, em_cut))
            ):
                source, target = mine if step == 0 else every.at[block], every.at[block]
                if step == half - 1:
                    cols = pl.ds(0, cut) if side == 0 else pl.ds(cut, mine.shape[1] - cut)
                    source, target = source.at[:, cols], target.at[:, cols]
                copies.append(
                    pltpu.make_async_remote_copy(
                        src_ref=source, dst_ref=target,
                        send_sem=ring_send.at[2 * side + kind, step],
                        recv_sem=ring_recv.at[2 * side + kind, step],
                        device_id={"dev": neighbour}, device_id_type=MESH,
                    )
                )
        return copies

    def pair_copies(spot, slot):
        block = index_of(spot)
        return [
            pltpu.make_async_remote_copy(
                src_ref=mine if slot == 0 else every.at[block], dst_ref=every.at[block],
                send_sem=pair_send.at[kind, slot], recv_sem=pair_recv.at[kind, slot],
                device_id={"rve": 1 - core}, device_id_type=MESH,
            )
            for kind, (mine, every) in enumerate(((up_ref, up_all), (em_ref, em_all)))
        ]

    def own_copies():
        block = index_of(place)
        return [
            pltpu.make_async_copy(mine, every.at[block], own_sem.at[kind])
            for kind, (mine, every) in enumerate(((up_ref, up_all), (em_ref, em_all)))
        ]

    pair_list = [(0, 0)]
    for step in range(half - 1):
        pair_list += [(-1 - step, 1 + 2 * step), (1 + step, 2 + 2 * step)]
    pair_list.append((half, 2 * half - 1))

    def gather_step(step):
        if step > 0:
            for copy in ring_copies(step - 1):
                copy.wait_recv()
        if step < half:
            for copy in ring_copies(step):
                copy.start()
        if step == 0:
            fresh = pair_list[:1]
        elif step < half:
            fresh = pair_list[2 * step - 1 : 2 * step + 1]
        else:
            fresh = pair_list[-1:]
        for shift, slot in fresh:
            for copy in pair_copies(place + shift, slot):
                copy.start()

    gather_step(0)
    for copy in own_copies():
        copy.start()

    labels[pl.ds(width, slab)] = phase_ref[...]

    @pl.when(dev == 0)
    def _():
        for row in range(width):
            labels[row] = phase_ref[0]

    @pl.when(dev == size - 1)
    def _():
        for row in range(width):
            labels[width + slab + row] = phase_ref[slab - 1]

    @pl.when(dev > 0)
    def _():
        halo(True).wait_recv()

    @pl.when(dev < size - 1)
    def _():
        halo(False).wait_recv()

    y_at = lax.broadcasted_iota(jnp.int32, (ny, nz), 0)
    z_at = lax.broadcasted_iota(jnp.int32, (ny, nz), 1)

    def inverse(row, kind):
        label = labels[row]
        value = jnp.full((ny, nz), inverse_ref[kind, phases - 1], jnp.float32)
        for phase in range(phases - 1):
            value = jnp.where(label == phase, inverse_ref[kind, phase], value)
        return value

    def within(row):
        spot = dev * slab - width + row
        at = jnp.full((ny, nz), spot, jnp.int32)
        return (at >= 0) & (at < grid_rows)

    def terms_row(row, carry):
        faces = []
        for kind in range(2):
            here = inverse(row, kind)
            upper_x = 2.0 / (here + inverse(row + 1, kind))
            lower_x = 2.0 / (here + inverse(row - 1, kind))
            upper_y = 2.0 / (here + jnp.where(y_at == ny - 1, here, pltpu.roll(here, ny - 1, 0)))
            lower_y = 2.0 / (here + jnp.where(y_at == 0, here, pltpu.roll(here, 1, 0)))
            upper_z = 2.0 / (here + jnp.where(z_at == nz - 1, here, pltpu.roll(here, nz - 1, 1)))
            lower_z = 2.0 / (here + jnp.where(z_at == 0, here, pltpu.roll(here, 1, 1)))
            face_x[2 * kind, row] = upper_x
            face_x[2 * kind + 1, row] = lower_x
            face_y[2 * kind, row] = jnp.where(y_at == ny - 1, 0.0, upper_y)
            face_y[2 * kind + 1, row] = jnp.where(y_at == 0, 0.0, lower_y)
            face_z[2 * kind, row] = jnp.where(z_at == nz - 1, 0.0, upper_z)
            face_z[2 * kind + 1, row] = jnp.where(z_at == 0, 0.0, lower_z)
            faces.append(
                [
                    (upper - lower, upper + lower)
                    for upper, lower in (
                        (upper_x, lower_x), (upper_y, lower_y), (upper_z, lower_z)
                    )
                ]
            )
        inside = within(row)
        for component in range(3):
            force = 0.0
            total = 0.0
            for direction in range(3):
                difference, both = faces[1 if direction == component else 0][direction]
                force = force + strain_ref[component, direction] * difference
                total = total + both
            back = jnp.where(inside, 1.0 / total, 0.0)
            forcing[component, row] = force
            scale_back[component, row] = back
            field[0, component, row] = force * back
        return carry

    def sweep(repeat):
        source, target = repeat % 2, (repeat + 1) % 2
        last = repeat == SWEEPS - 2

        def sweep_row(row, carry):
            for component in range(3):
                kinds = [2 if direction == component else 0 for direction in range(3)]
                here = field[source, component, row]
                total = forcing[component, row]
                total = total + face_x[kinds[0], row] * field[source, component, row + 1]
                total = total + face_x[kinds[0] + 1, row] * field[source, component, row - 1]
                total = total + face_y[kinds[1], row] * pltpu.roll(here, ny - 1, 0)
                total = total + face_y[kinds[1] + 1, row] * pltpu.roll(here, 1, 0)
                total = total + face_z[kinds[2], row] * pltpu.roll(here, nz - 1, 1)
                total = total + face_z[kinds[2] + 1, row] * pltpu.roll(here, 1, 1)
                result = total * scale_back[component, row]
                if last:
                    disp_ref[component, row - width] = result
                else:
                    field[target, component, row] = result
            return carry

        lax.fori_loop(2 + repeat, slab + 2 * width - 2 - repeat, sweep_row, 0)

    lax.fori_loop(1, slab + 2 * width - 1, terms_row, 0)
    gather_step(1)
    sweep(0)
    sweep(1)
    gather_step(2)
    sweep(2)

    bands = ny // PATCH_Y // size
    piece = 3 * slab * PATCH_Y

    for dest in range(size):
        for band in range(bands):
            first = (dest * bands + band) * PATCH_Y
            rows = disp_ref[:, :, first : first + PATCH_Y, :].reshape(piece, nz)
            outgo[dest, band * piece : (band + 1) * piece] = rows.astype(jnp.bfloat16)

    def swap_copy(offset):
        dest = (dev + offset) % size
        return pltpu.make_async_remote_copy(
            src_ref=outgo.at[dest], dst_ref=income.at[dev],
            send_sem=swap_send.at[offset], recv_sem=swap_recv.at[offset],
            device_id={"dev": dest}, device_id_type=MESH,
        )

    for offset in range(1, size):
        swap_copy(offset).start()
    income[dev] = outgo[dev]
    for step in range(3, half):
        gather_step(step)
    for offset in range(1, size):
        swap_copy(offset).wait_recv()

    cells = nz // PATCH_Z
    joined = LANES // cells
    depth = joined * nz
    from_row = lax.broadcasted_iota(jnp.int32, (depth, LANES), 0)
    to_lane = lax.broadcasted_iota(jnp.int32, (depth, LANES), 1)
    base = (to_lane // cells) * nz + (to_lane % cells) * PATCH_Z
    for band in range(bands):
        for group in range(size // joined):
            rows = jnp.concatenate(
                [
                    income[group * joined + member, band * piece : (band + 1) * piece]
                    for member in range(joined)
                ],
                axis=1,
            )
            lane = band * size * cells + group * LANES
            for part in range(PATCH_Z):
                pick = jnp.where(from_row == base + part, 1.0, 0.0).astype(jnp.bfloat16)
                sorted_rows[part * piece : (part + 1) * piece, lane : lane + LANES] = jnp.dot(
                    rows, pick, preferred_element_type=jnp.float32
                ).astype(jnp.bfloat16)
    features = PATCH_Z * piece
    to_row = lax.broadcasted_iota(jnp.int32, (features, features), 0)
    from_col = lax.broadcasted_iota(jnp.int32, (features, features), 1)
    order = (to_row % PATCH_Z) * piece + to_row // PATCH_Z
    move = jnp.where(from_col == order, 1.0, 0.0).astype(jnp.bfloat16)
    patch_ref[...] = jnp.dot(
        move, sorted_rows[...], preferred_element_type=jnp.float32
    ).astype(jnp.bfloat16)

    gather_step(half)

    @pl.when(dev < size - 1)
    def _():
        halo(True).wait_send()

    @pl.when(dev > 0)
    def _():
        halo(False).wait_send()

    for copy in own_copies():
        copy.wait()
    for step in range(half):
        for copy in ring_copies(step):
            copy.wait_send()
    for shift, slot in pair_list:
        for copy in pair_copies(place + shift, slot):
            copy.wait()
    for offset in range(1, size):
        swap_copy(offset).wait_send()


def fields_and_gathers(phase, inverse, strain, w_embed, w_up, size):
    slab, ny, nz = phase.shape
    rows = slab + 2 * SWEEPS
    bands = ny // PATCH_Y // size
    piece = 3 * slab * PATCH_Y
    features = PATCH_Z * piece
    tokens = bands * size * (nz // PATCH_Z)
    wide = jnp.float32
    half = size // 2
    plane = (rows, ny, nz)
    vmem = pl.BlockSpec(memory_space=pltpu.VMEM)
    smem = pl.BlockSpec(memory_space=pltpu.SMEM)
    far = pl.BlockSpec(memory_space=pl.ANY)
    return pl.pallas_call(
        partial(field_kernel, size, slab * size),
        out_shape=(
            jax.ShapeDtypeStruct((3, slab, ny, nz), wide),
            jax.ShapeDtypeStruct((features, tokens), jnp.bfloat16),
            jax.ShapeDtypeStruct((2 * size,) + w_up.shape, w_up.dtype),
            jax.ShapeDtypeStruct((2 * size,) + w_embed.shape, w_embed.dtype),
        ),
        in_specs=[vmem, smem, smem, far, far],
        out_specs=(vmem, vmem, far, far),
        scratch_shapes=[
            pltpu.VMEM(plane, jnp.int32),
            pltpu.VMEM((4,) + plane, wide),
            pltpu.VMEM((4,) + plane, wide),
            pltpu.VMEM((4,) + plane, wide),
            pltpu.VMEM((3,) + plane, wide),
            pltpu.VMEM((3,) + plane, wide),
            pltpu.VMEM((2, 3) + plane, wide),
            pltpu.VMEM((size, bands * piece, nz), jnp.bfloat16),
            pltpu.VMEM((size, bands * piece, nz), jnp.bfloat16),
            pltpu.VMEM((features, tokens), jnp.bfloat16),
            pltpu.SemaphoreType.DMA((2,)),
            pltpu.SemaphoreType.DMA((2,)),
            pltpu.SemaphoreType.DMA((4, half)),
            pltpu.SemaphoreType.DMA((4, half)),
            pltpu.SemaphoreType.DMA((2, size)),
            pltpu.SemaphoreType.DMA((2, size)),
            pltpu.SemaphoreType.DMA((2,)),
            pltpu.SemaphoreType.DMA((size,)),
            pltpu.SemaphoreType.DMA((size,)),
        ],
        compiler_params=pltpu.CompilerParams(
            collective_id=1, has_side_effects=True, vmem_limit_bytes=58 * 1024 * 1024
        ),
        cost_estimate=pl.CostEstimate(
            flops=2_000_000_000, bytes_accessed=30_000_000, transcendentals=0
        ),
    )(phase, inverse, strain, w_up, w_embed)


def learner(patches, embed_all, up_all, cotangent, dev_count, rve_count):
    tokens = patches.shape[1]
    shards = dev_count * rve_count
    grad_scale = 1.0 / math.sqrt(tokens * shards)
    embedded = jnp.dot(embed_all, patches, preferred_element_type=jnp.float32).astype(jnp.bfloat16)
    embed_wide = embedded.astype(jnp.float32)
    inverse_rms = lax.rsqrt(jnp.mean(embed_wide * embed_wide, axis=0, keepdims=True) + epsilon)
    normed_wide = embed_wide * inverse_rms
    normed = normed_wide.astype(jnp.bfloat16)
    pre_act = jnp.dot(up_all, normed, preferred_element_type=jnp.float32)
    act_grad = gelu_grad(pre_act, cotangent)
    normed_grad = lax.dot_general(
        up_all, act_grad, (((0,), (0,)), ((), ())), preferred_element_type=jnp.float32
    )
    embed_in_grad = (
        inverse_rms
        * (normed_grad - normed_wide * jnp.mean(normed_grad * normed_wide, axis=0, keepdims=True))
    ).astype(jnp.bfloat16)
    grad_up, grad_embed = scatter_grads(
        act_grad.reshape(shards, -1, tokens),
        normed,
        embed_in_grad.reshape(shards, -1, tokens),
        patches,
        grad_scale,
        dev_count,
    )
    return (grad_embed, grad_up)


def local(phase, load_case, moduli, loading_table, w_embed, w_up, cotangent):
    dev_count = lax.axis_size("dev")
    rve_count = lax.axis_size("rve")
    case_labels = jnp.arange(loading_table.shape[0], dtype=jnp.int32)
    case_pick = (case_labels == load_case[0]).astype(jnp.float32)
    strain = jnp.sum(case_pick[:, None, None] * loading_table, axis=0)
    displace, patches, up_all, embed_all = fields_and_gathers(
        phase[0], 1.0 / moduli, strain, w_embed, w_up, dev_count
    )
    return (displace[None],) + learner(
        patches,
        embed_all.reshape(-1, w_embed.shape[1]),
        up_all.reshape(-1, w_up.shape[1]),
        cotangent.T,
        dev_count,
        rve_count,
    )


def solution(mesh):
    return jax.shard_map(
        local,
        mesh=mesh,
        in_specs=(
            P(("groups", "rve"), "dev", None, None),
            P(("groups", "rve")),
            P(),
            P(),
            P(("dev", "rve"), None),
            P(("dev", "rve"), None),
            P(("groups", "dev", "rve"), None),
        ),
        out_specs=(
            P(("groups", "rve"), None, "dev", None, None),
            P(("groups", "dev", "rve"), None),
            P(("groups", "dev", "rve"), None),
        ),
        check_vma=False,
    )
```

```python
from functools import partial
import math

import jax
import jax.numpy as jnp
from jax import lax
from jax.experimental import pallas as pl
from jax.experimental.pallas import tpu as pltpu
from jax.sharding import PartitionSpec as P

PATCH_X = 8
PATCH_Y = 8
PATCH_Z = 4
SWEEPS = 4


epsilon = 1e-06


MESH = pl.DeviceIdType.MESH
LANES = 128


def dot_last(left, right):
    return lax.dot_general(
        left, right, (((1,), (1,)), ((), ())), preferred_element_type=jnp.float32
    )


def ring_place(dev, size):
    odd = dev % 2
    return (1 - odd) * (dev // 2) + odd * (size - 1 - dev // 2)


def ring_dev(place, size):
    back = place // (size // 2)
    return (1 - back) * (2 * place) + back * (2 * (size - 1 - place) + 1)


def scatter_kernel(
    size, scale, up_cut, embed_cut,
    act_ref, normed_ref, embed_ref, patch_ref, up_out, embed_out,
    own_up, own_em, pair_out_up, pair_out_em, pair_in_up, pair_in_em,
    ring_out_up, ring_out_em, ring_in_up, ring_in_em,
    pair_send, pair_recv, ring_send, ring_recv,
):
    dev = lax.axis_index("dev")
    core = lax.axis_index("rve")
    place = ring_place(dev, size)
    right = ring_dev((place + 1) % size, size)
    left = ring_dev((place + size - 1) % size, size)
    barrier = pltpu.get_barrier_semaphore()
    pl.semaphore_signal(barrier, inc=1, device_id={"dev": right}, device_id_type=MESH)
    pl.semaphore_signal(barrier, inc=1, device_id={"dev": left}, device_id_type=MESH)
    pl.semaphore_signal(barrier, inc=1, device_id={"rve": 1 - core}, device_id_type=MESH)
    pl.semaphore_wait(barrier, 3)
    sides = (
        (slice(0, up_cut), slice(0, embed_cut)),
        (slice(up_cut, None), slice(embed_cut, None)),
    )

    def pair_copies(step):
        return [
            pltpu.make_async_remote_copy(
                src_ref=source.at[step], dst_ref=target.at[step],
                send_sem=pair_send.at[kind, step], recv_sem=pair_recv.at[kind, step],
                device_id={"rve": 1 - core}, device_id_type=MESH,
            )
            for kind, (source, target) in enumerate(
                ((pair_out_up, pair_in_up), (pair_out_em, pair_in_em))
            )
        ]

    up_width, em_width = normed_ref.shape[0], patch_ref.shape[0]
    first_mid = (up_cut // LANES + 1) // 2 * LANES
    other_mid = up_cut + ((up_width - up_cut) // LANES + 1) // 2 * LANES
    up_buffers = (own_up, pair_in_up, ring_in_up, ring_out_up, up_out)
    em_buffers = (own_em, pair_in_em, ring_in_em, ring_out_em, embed_out)
    chunks = (
        (0, up_buffers, slice(0, first_mid)),
        (1, up_buffers, slice(up_cut, other_mid)),
        (0, up_buffers, slice(first_mid, up_cut)),
        (1, up_buffers, slice(other_mid, up_width)),
        (0, em_buffers, slice(0, embed_cut)),
        (1, em_buffers, slice(embed_cut, em_width)),
    )

    def ring_copies(step):
        return [
            pltpu.make_async_remote_copy(
                src_ref=buffers[3].at[step, :, cols], dst_ref=buffers[2].at[step, :, cols],
                send_sem=ring_send.at[number, step], recv_sem=ring_recv.at[number, step],
                device_id={"dev": (right, left)[side]}, device_id_type=MESH,
            )
            for number, (side, buffers, cols) in enumerate(chunks)
        ]

    def compute(step):
        blocks = ((place + 2 * size - 1 - step) % size, (place + 1 + step) % size)
        for other in (True, False):
            for side in range(2):
                up_cols, em_cols = sides[side]
                block = ring_dev(blocks[side], size) * 2 + ((1 - core) if other else core)
                up = dot_last(act_ref[block], normed_ref[up_cols])
                em = dot_last(embed_ref[block], patch_ref[em_cols])
                if other:
                    pair_out_up[step, :, up_cols] = up.astype(jnp.bfloat16)
                    pair_out_em[step, :, em_cols] = em.astype(jnp.bfloat16)
                else:
                    own_up[step % 2, :, up_cols] = up
                    own_em[step % 2, :, em_cols] = em
            if other:
                for copy in pair_copies(step):
                    copy.start()

    def finish(step, first, last):
        for copy in pair_copies(step):
            copy.wait_recv()
        before = None if first else ring_copies(step - 1)
        after = None if last else ring_copies(step)
        for number, (side, buffers, cols) in enumerate(chunks):
            own, pair_in, ring_in, ring_out, result = buffers
            total = own[step % 2, :, cols] + pair_in[step, :, cols].astype(jnp.float32)
            if not first:
                before[number].wait_recv()
                total = total + ring_in[step - 1, :, cols].astype(jnp.float32)
            if last:
                result[:, cols] = total * scale
            else:
                ring_out[step, :, cols] = total.astype(jnp.bfloat16)
                after[number].start()

    compute(0)
    compute(1)
    finish(0, True, False)

    def body(step, carry):
        compute(step + 1)
        finish(step, False, False)
        return carry

    lax.fori_loop(1, size - 1, body, 0)
    finish(size - 1, False, True)

    def drain(step, carry):
        for copy in pair_copies(step):
            copy.wait_send()
        return carry

    def drain_ring(step, carry):
        for copy in ring_copies(step):
            copy.wait_send()
        return carry

    lax.fori_loop(0, size, drain, 0)
    lax.fori_loop(0, size - 1, drain_ring, 0)


def scatter_grads(act, normed, embed, patches, scale, size):
    up_rows, em_rows = act.shape[1], embed.shape[1]
    width, features = normed.shape[0], patches.shape[0]
    up_cut = (width // LANES + 1) // 2 * LANES
    embed_cut = features // LANES // 3 * LANES
    wide = jnp.bfloat16
    return pl.pallas_call(
        partial(scatter_kernel, size, scale, up_cut, embed_cut),
        out_shape=(
            jax.ShapeDtypeStruct((up_rows, width), jnp.float32),
            jax.ShapeDtypeStruct((em_rows, features), jnp.float32),
        ),
        in_specs=[pl.BlockSpec(memory_space=pltpu.VMEM)] * 4,
        out_specs=(pl.BlockSpec(memory_space=pltpu.VMEM),) * 2,
        scratch_shapes=[
            pltpu.VMEM((2, up_rows, width), jnp.float32),
            pltpu.VMEM((2, em_rows, features), jnp.float32),
            *[
                pltpu.VMEM(shape, wide)
                for _ in range(4)
                for shape in ((size, up_rows, width), (size, em_rows, features))
            ],
            pltpu.SemaphoreType.DMA((2, size)),
            pltpu.SemaphoreType.DMA((2, size)),
            pltpu.SemaphoreType.DMA((6, size)),
            pltpu.SemaphoreType.DMA((6, size)),
        ],
        compiler_params=pltpu.CompilerParams(
            collective_id=0, has_side_effects=True, vmem_limit_bytes=58 * 1024 * 1024
        ),
        cost_estimate=pl.CostEstimate(
            flops=4 * size * patches.shape[1] * (up_rows * width + em_rows * features),
            bytes_accessed=20_000_000,
            transcendentals=0,
        ),
    )(act, normed, embed, patches)


def gelu_grad(pre_act, cotangent):
    _, pullback = jax.vjp(partial(jax.nn.gelu, approximate=True), pre_act)
    return pullback(cotangent.astype(jnp.float32))[0].astype(jnp.bfloat16)


def field_kernel(
    size, grid_rows, phase_ref, inverse_ref, strain_ref, up_ref, em_ref,
    disp_ref, patch_ref, up_all, em_all,
    labels, face_x, face_y, face_z, forcing, scale_back, field, outgo, income, sorted_rows,
    halo_send, halo_recv, ring_send, ring_recv, pair_send, pair_recv, own_sem, swap_send, swap_recv,
):
    slab, ny, nz = phase_ref.shape
    width = SWEEPS
    phases = inverse_ref.shape[1]
    dev = lax.axis_index("dev")
    core = lax.axis_index("rve")
    place = ring_place(dev, size)
    right = ring_dev((place + 1) % size, size)
    left = ring_dev((place + size - 1) % size, size)
    half = size // 2
    up_cut = (up_ref.shape[1] // LANES + 1) // 2 * LANES
    em_cut = em_ref.shape[1] // LANES // 3 * LANES

    barrier = pltpu.get_barrier_semaphore()
    for offset in range(1, size):
        pl.semaphore_signal(
            barrier, inc=1, device_id={"dev": (dev + offset) % size}, device_id_type=MESH
        )
    pl.semaphore_signal(barrier, inc=1, device_id={"rve": 1 - core}, device_id_type=MESH)
    pl.semaphore_wait(barrier, size)

    def halo(up):
        if up:
            source, target = phase_ref.at[pl.ds(slab - width, width)], labels.at[pl.ds(0, width)]
        else:
            source, target = phase_ref.at[pl.ds(0, width)], labels.at[pl.ds(width + slab, width)]
        way = 0 if up else 1
        return pltpu.make_async_remote_copy(
            src_ref=source, dst_ref=target, send_sem=halo_send.at[way], recv_sem=halo_recv.at[way],
            device_id={"dev": (dev + 1) % size if up else (dev + size - 1) % size},
            device_id_type=MESH,
        )

    @pl.when(dev < size - 1)
    def _():
        halo(True).start()

    @pl.when(dev > 0)
    def _():
        halo(False).start()

    def index_of(spot):
        return ring_dev((spot + 2 * size) % size, size) * 2 + core

    wide_end, em_end = up_ref.shape[1], em_ref.shape[1]

    def pieces(step, side):
        if step < half - 1:
            return ((0, 0, 0, up_cut), (1, 0, up_cut, wide_end), (2, 1, 0, em_end))
        if side == 0:
            return ((0, 0, 0, up_cut), (2, 1, 0, em_cut))
        return ((1, 0, up_cut, wide_end), (2, 1, em_cut, em_end))

    def ring_copies(step):
        copies = {}
        for side, neighbour in enumerate((right, left)):
            block = index_of(place - step if side == 0 else place + step)
            for chunk, kind, first, end in pieces(step, side):
                mine, every = ((up_ref, up_all), (em_ref, em_all))[kind]
                cols = pl.ds(first, end - first)
                source = mine if step == 0 else every.at[block]
                copies[chunk, side] = pltpu.make_async_remote_copy(
                    src_ref=source.at[:, cols], dst_ref=every.at[block, :, cols],
                    send_sem=ring_send.at[3 * side + chunk, step],
                    recv_sem=ring_recv.at[3 * side + chunk, step],
                    device_id={"dev": neighbour}, device_id_type=MESH,
                )
        return copies

    def pair_copies(spot, slot):
        block = index_of(spot)
        return [
            pltpu.make_async_remote_copy(
                src_ref=mine if slot == 0 else every.at[block], dst_ref=every.at[block],
                send_sem=pair_send.at[kind, slot], recv_sem=pair_recv.at[kind, slot],
                device_id={"rve": 1 - core}, device_id_type=MESH,
            )
            for kind, (mine, every) in enumerate(((up_ref, up_all), (em_ref, em_all)))
        ]

    def own_copies():
        block = index_of(place)
        return [
            pltpu.make_async_copy(mine, every.at[block], own_sem.at[kind])
            for kind, (mine, every) in enumerate(((up_ref, up_all), (em_ref, em_all)))
        ]

    pair_list = [(0, 0)]
    for step in range(half - 1):
        pair_list += [(-1 - step, 1 + 2 * step), (1 + step, 2 + 2 * step)]
    pair_list.append((half, 2 * half - 1))

    def gather_step(step):
        before = ring_copies(step - 1) if step > 0 else {}
        after = ring_copies(step) if step < half else {}
        for chunk in range(3):
            for side in range(2):
                if (chunk, side) in before:
                    before[chunk, side].wait_recv()
                if (chunk, side) in after:
                    after[chunk, side].start()
        if step == 0:
            fresh = pair_list[:1]
        elif step < half:
            fresh = pair_list[2 * step - 1 : 2 * step + 1]
        else:
            fresh = pair_list[-1:]
        for shift, slot in fresh:
            for copy in pair_copies(place + shift, slot):
                copy.start()

    gather_step(0)
    for copy in own_copies():
        copy.start()

    labels[pl.ds(width, slab)] = phase_ref[...]

    @pl.when(dev == 0)
    def _():
        for row in range(width):
            labels[row] = phase_ref[0]

    @pl.when(dev == size - 1)
    def _():
        for row in range(width):
            labels[width + slab + row] = phase_ref[slab - 1]

    @pl.when(dev > 0)
    def _():
        halo(True).wait_recv()

    @pl.when(dev < size - 1)
    def _():
        halo(False).wait_recv()

    y_at = lax.broadcasted_iota(jnp.int32, (ny, nz), 0)
    z_at = lax.broadcasted_iota(jnp.int32, (ny, nz), 1)

    def inverse(row, kind):
        label = labels[row]
        value = jnp.full((ny, nz), inverse_ref[kind, phases - 1], jnp.float32)
        for phase in range(phases - 1):
            value = jnp.where(label == phase, inverse_ref[kind, phase], value)
        return value

    def within(row):
        spot = dev * slab - width + row
        at = jnp.full((ny, nz), spot, jnp.int32)
        return (at >= 0) & (at < grid_rows)

    def terms_row(row, carry):
        faces = []
        for kind in range(2):
            here = inverse(row, kind)
            upper_x = 2.0 / (here + inverse(row + 1, kind))
            lower_x = 2.0 / (here + inverse(row - 1, kind))
            upper_y = 2.0 / (here + jnp.where(y_at == ny - 1, here, pltpu.roll(here, ny - 1, 0)))
            lower_y = 2.0 / (here + jnp.where(y_at == 0, here, pltpu.roll(here, 1, 0)))
            upper_z = 2.0 / (here + jnp.where(z_at == nz - 1, here, pltpu.roll(here, nz - 1, 1)))
            lower_z = 2.0 / (here + jnp.where(z_at == 0, here, pltpu.roll(here, 1, 1)))
            face_x[2 * kind, row] = upper_x
            face_x[2 * kind + 1, row] = lower_x
            face_y[2 * kind, row] = jnp.where(y_at == ny - 1, 0.0, upper_y)
            face_y[2 * kind + 1, row] = jnp.where(y_at == 0, 0.0, lower_y)
            face_z[2 * kind, row] = jnp.where(z_at == nz - 1, 0.0, upper_z)
            face_z[2 * kind + 1, row] = jnp.where(z_at == 0, 0.0, lower_z)
            faces.append(
                [
                    (upper - lower, upper + lower)
                    for upper, lower in (
                        (upper_x, lower_x), (upper_y, lower_y), (upper_z, lower_z)
                    )
                ]
            )
        inside = within(row)
        for component in range(3):
            force = 0.0
            total = 0.0
            for direction in range(3):
                difference, both = faces[1 if direction == component else 0][direction]
                force = force + strain_ref[component, direction] * difference
                total = total + both
            back = jnp.where(inside, 1.0 / total, 0.0)
            forcing[component, row] = force
            scale_back[component, row] = back
            field[0, component, row] = force * back
        return carry

    def sweep(repeat):
        source, target = repeat % 2, (repeat + 1) % 2
        last = repeat == SWEEPS - 2

        def sweep_row(row, carry):
            for component in range(3):
                kinds = [2 if direction == component else 0 for direction in range(3)]
                here = field[source, component, row]
                total = forcing[component, row]
                total = total + face_x[kinds[0], row] * field[source, component, row + 1]
                total = total + face_x[kinds[0] + 1, row] * field[source, component, row - 1]
                total = total + face_y[kinds[1], row] * pltpu.roll(here, ny - 1, 0)
                total = total + face_y[kinds[1] + 1, row] * pltpu.roll(here, 1, 0)
                total = total + face_z[kinds[2], row] * pltpu.roll(here, nz - 1, 1)
                total = total + face_z[kinds[2] + 1, row] * pltpu.roll(here, 1, 1)
                result = total * scale_back[component, row]
                if last:
                    disp_ref[component, row - width] = result
                else:
                    field[target, component, row] = result
            return carry

        lax.fori_loop(2 + repeat, slab + 2 * width - 2 - repeat, sweep_row, 0)

    lax.fori_loop(1, slab + 2 * width - 1, terms_row, 0)
    gather_step(1)
    sweep(0)
    sweep(1)
    sweep(2)

    bands = ny // PATCH_Y // size
    piece = 3 * slab * PATCH_Y

    for dest in range(size):
        for band in range(bands):
            first = (dest * bands + band) * PATCH_Y
            rows = disp_ref[:, :, first : first + PATCH_Y, :].reshape(piece, nz)
            outgo[dest, band * piece : (band + 1) * piece] = rows.astype(jnp.bfloat16)

    def swap_copy(offset):
        dest = (dev + offset) % size
        return pltpu.make_async_remote_copy(
            src_ref=outgo.at[dest], dst_ref=income.at[dev],
            send_sem=swap_send.at[offset], recv_sem=swap_recv.at[offset],
            device_id={"dev": dest}, device_id_type=MESH,
        )

    for offset in range(1, size):
        swap_copy(offset).start()
    income[dev] = outgo[dev]
    for step in range(2, half):
        gather_step(step)
    for offset in range(1, size):
        swap_copy(offset).wait_recv()

    cells = nz // PATCH_Z
    joined = LANES // cells
    depth = joined * nz
    from_row = lax.broadcasted_iota(jnp.int32, (depth, LANES), 0)
    to_lane = lax.broadcasted_iota(jnp.int32, (depth, LANES), 1)
    base = (to_lane // cells) * nz + (to_lane % cells) * PATCH_Z
    for band in range(bands):
        for group in range(size // joined):
            rows = jnp.concatenate(
                [
                    income[group * joined + member, band * piece : (band + 1) * piece]
                    for member in range(joined)
                ],
                axis=1,
            )
            lane = band * size * cells + group * LANES
            for part in range(PATCH_Z):
                pick = jnp.where(from_row == base + part, 1.0, 0.0).astype(jnp.bfloat16)
                sorted_rows[part * piece : (part + 1) * piece, lane : lane + LANES] = jnp.dot(
                    rows, pick, preferred_element_type=jnp.float32
                ).astype(jnp.bfloat16)
    features = PATCH_Z * piece
    to_row = lax.broadcasted_iota(jnp.int32, (features, features), 0)
    from_col = lax.broadcasted_iota(jnp.int32, (features, features), 1)
    order = (to_row % PATCH_Z) * piece + to_row // PATCH_Z
    move = jnp.where(from_col == order, 1.0, 0.0).astype(jnp.bfloat16)
    patch_ref[...] = jnp.dot(
        move, sorted_rows[...], preferred_element_type=jnp.float32
    ).astype(jnp.bfloat16)

    gather_step(half)

    @pl.when(dev < size - 1)
    def _():
        halo(True).wait_send()

    @pl.when(dev > 0)
    def _():
        halo(False).wait_send()

    for copy in own_copies():
        copy.wait()
    for step in range(half):
        for copy in ring_copies(step).values():
            copy.wait_send()
    for shift, slot in pair_list:
        for copy in pair_copies(place + shift, slot):
            copy.wait()
    for offset in range(1, size):
        swap_copy(offset).wait_send()


def fields_and_gathers(phase, inverse, strain, w_embed, w_up, size):
    slab, ny, nz = phase.shape
    rows = slab + 2 * SWEEPS
    bands = ny // PATCH_Y // size
    piece = 3 * slab * PATCH_Y
    features = PATCH_Z * piece
    tokens = bands * size * (nz // PATCH_Z)
    wide = jnp.float32
    half = size // 2
    plane = (rows, ny, nz)
    vmem = pl.BlockSpec(memory_space=pltpu.VMEM)
    smem = pl.BlockSpec(memory_space=pltpu.SMEM)
    far = pl.BlockSpec(memory_space=pl.ANY)
    return pl.pallas_call(
        partial(field_kernel, size, slab * size),
        out_shape=(
            jax.ShapeDtypeStruct((3, slab, ny, nz), wide),
            jax.ShapeDtypeStruct((features, tokens), jnp.bfloat16),
            jax.ShapeDtypeStruct((2 * size,) + w_up.shape, w_up.dtype),
            jax.ShapeDtypeStruct((2 * size,) + w_embed.shape, w_embed.dtype),
        ),
        in_specs=[vmem, smem, smem, far, far],
        out_specs=(vmem, vmem, far, far),
        scratch_shapes=[
            pltpu.VMEM(plane, jnp.int32),
            pltpu.VMEM((4,) + plane, wide),
            pltpu.VMEM((4,) + plane, wide),
            pltpu.VMEM((4,) + plane, wide),
            pltpu.VMEM((3,) + plane, wide),
            pltpu.VMEM((3,) + plane, wide),
            pltpu.VMEM((2, 3) + plane, wide),
            pltpu.VMEM((size, bands * piece, nz), jnp.bfloat16),
            pltpu.VMEM((size, bands * piece, nz), jnp.bfloat16),
            pltpu.VMEM((features, tokens), jnp.bfloat16),
            pltpu.SemaphoreType.DMA((2,)),
            pltpu.SemaphoreType.DMA((2,)),
            pltpu.SemaphoreType.DMA((6, half)),
            pltpu.SemaphoreType.DMA((6, half)),
            pltpu.SemaphoreType.DMA((2, size)),
            pltpu.SemaphoreType.DMA((2, size)),
            pltpu.SemaphoreType.DMA((2,)),
            pltpu.SemaphoreType.DMA((size,)),
            pltpu.SemaphoreType.DMA((size,)),
        ],
        compiler_params=pltpu.CompilerParams(
            collective_id=1, has_side_effects=True, vmem_limit_bytes=58 * 1024 * 1024
        ),
        cost_estimate=pl.CostEstimate(
            flops=2_000_000_000, bytes_accessed=30_000_000, transcendentals=0
        ),
    )(phase, inverse, strain, w_up, w_embed)


def learner(patches, embed_all, up_all, cotangent, dev_count, rve_count):
    tokens = patches.shape[1]
    shards = dev_count * rve_count
    grad_scale = 1.0 / math.sqrt(tokens * shards)
    embedded = jnp.dot(embed_all, patches, preferred_element_type=jnp.float32).astype(jnp.bfloat16)
    embed_wide = embedded.astype(jnp.float32)
    inverse_rms = lax.rsqrt(jnp.mean(embed_wide * embed_wide, axis=0, keepdims=True) + epsilon)
    normed_wide = embed_wide * inverse_rms
    normed = normed_wide.astype(jnp.bfloat16)
    pre_act = jnp.dot(up_all, normed, preferred_element_type=jnp.float32)
    act_grad = gelu_grad(pre_act, cotangent)
    normed_grad = lax.dot_general(
        up_all, act_grad, (((0,), (0,)), ((), ())), preferred_element_type=jnp.float32
    )
    embed_in_grad = (
        inverse_rms
        * (normed_grad - normed_wide * jnp.mean(normed_grad * normed_wide, axis=0, keepdims=True))
    ).astype(jnp.bfloat16)
    grad_up, grad_embed = scatter_grads(
        act_grad.reshape(shards, -1, tokens),
        normed,
        embed_in_grad.reshape(shards, -1, tokens),
        patches,
        grad_scale,
        dev_count,
    )
    return (grad_embed, grad_up)


def local(phase, load_case, moduli, loading_table, w_embed, w_up, cotangent):
    dev_count = lax.axis_size("dev")
    rve_count = lax.axis_size("rve")
    case_labels = jnp.arange(loading_table.shape[0], dtype=jnp.int32)
    case_pick = (case_labels == load_case[0]).astype(jnp.float32)
    strain = jnp.sum(case_pick[:, None, None] * loading_table, axis=0)
    displace, patches, up_all, embed_all = fields_and_gathers(
        phase[0], 1.0 / moduli, strain, w_embed, w_up, dev_count
    )
    return (displace[None],) + learner(
        patches,
        embed_all.reshape(-1, w_embed.shape[1]),
        up_all.reshape(-1, w_up.shape[1]),
        cotangent.T,
        dev_count,
        rve_count,
    )


def solution(mesh):
    return jax.shard_map(
        local,
        mesh=mesh,
        in_specs=(
            P(("groups", "rve"), "dev", None, None),
            P(("groups", "rve")),
            P(),
            P(),
            P(("dev", "rve"), None),
            P(("dev", "rve"), None),
            P(("groups", "dev", "rve"), None),
        ),
        out_specs=(
            P(("groups", "rve"), None, "dev", None, None),
            P(("groups", "dev", "rve"), None),
            P(("groups", "dev", "rve"), None),
        ),
        check_vma=False,
    )
```
